32 devices in a mesh: rep: 8 (over z, y), exp: 4 (over x, core).
Axes of the slice: x: 2, y: 2, z: 4, core: 2. Of those that a mesh axis runs over, the one named last changes fastest.
Arguments:
- tokens: bfloat16 [4096, 2048], P(('rep', 'exp')), may hold values from -6 to 6
- attend_weight: bfloat16 [2048, 16, 256], P(None, 'exp'), may hold values from -0.125 to 0.125
- value_weight: bfloat16 [2048, 32, 256], P(None, 'exp'), may hold values from -0.125 to 0.125
- rate_weight: bfloat16 [2048, 32, 2], P(None, 'exp'), may hold values from -0.125 to 0.125
- decay_rate: float32 [32], P('exp'), may hold values from 0.002 to 0.2
- output_weight: bfloat16 [32, 128, 2048], P('exp'), may hold values from -0.09375 to 0.09375
- state_cache: float32 [64, 32, 128, 128], P('rep', 'exp'), may hold values from -2.4 to 2.4
- resume_from: int32 [64], replicated, may hold values from 0 to 63, as said below
- expert_index: int32 [4096, 2], P(('rep', 'exp')), may hold values from 0 to 3, all different within a row; in each aligned block of 128 rows (0 to 127, 128 to 255, ...) at most 128 rows name the same one
- route_weight: float32 [4096, 2], P(('rep', 'exp')), may hold values from 0.02 to 0.3
- expert_inner: bfloat16 [4, 2048, 1024], P('exp'), may hold values from -0.125 to 0.125
- expert_outer: bfloat16 [4, 512, 2048], P('exp'), may hold values from -0.25 to 0.25
Outputs:
- layer_output: bfloat16 [4096, 2048], P(('rep', 'exp'))
- final_state: float32 [64, 32, 128, 128], P('rep', 'exp')
The draws below stay inside these ranges and needn't reach their ends.
Inputs may be any that keep to these rules, and one draw needn't show every extreme that they name: `resume_from`: entry r * 8 + b is the cache row of trajectory b of group r; cache row c belongs to group c // 8. The 8 trajectories of one group take their rows from 8 different groups; a row may serve several groups. `expert_index`: each row names 2 different experts.
All inputs are finite; a program needn't handle non-finite values.
Results may differ from the reference program's by a relative error of at most 0.013.
Values may be sent and summed in bfloat16 or wider, within the bound.
A program may use at most 128 MiB of HBM per device.

```python
import math
import jax
import jax.numpy as jnp
import numpy as np
from jax import lax

D = 2048
KHEADS = 16
VHEADS = 32
DK = 128
DV = 128
MI = 512
TRAJ = 8
LEN = 64
EXPERTS = 4
TOP = 2
ROWS = 128
TOKENS = 4096
N_REP = 8


def draw_resume_from(key, part):
    favoured = (jax.random.randint(jax.random.fold_in(key, 7), (N_REP,), 0, 4) == 0).astype(jnp.int32)

    def one_group(number):
        group_key = jax.random.fold_in(jax.random.fold_in(key, 11), number)
        key_order, key_place, key_slot = jax.random.split(group_key, 3)
        scores = jax.random.randint(key_order, (N_REP,), 0, 1000) - 700 * favoured
        ranking = jnp.argsort(scores * N_REP + jnp.arange(N_REP, dtype=jnp.int32))
        sources = ranking[:TRAJ].astype(jnp.int32)
        sources = sources[jax.random.permutation(key_place, TRAJ)]
        slot_rows = jax.random.randint(key_slot, (TRAJ,), 0, TRAJ)
        return (sources * TRAJ + slot_rows).astype(jnp.int32)
    return jax.vmap(one_group)(jnp.arange(N_REP, dtype=jnp.int32)).reshape(-1)


def shard_levels(stream_key, extent, cuts, low, largest):
    factor_of, own = 1.0, jax.random.fold_in(stream_key, 6)
    for axis_at, parts in cuts:
        heights = jnp.exp(jax.random.uniform(jax.random.fold_in(own, axis_at), (parts,), jnp.float32, low / len(cuts), largest / len(cuts)))
        factor_of = factor_of * jnp.repeat(heights, extent[axis_at] // parts).reshape([-1 if axis == axis_at else 1 for axis in range(len(extent))])
    return factor_of


def routed_block(own_key, own, number, rows, count, top, reach, lean):
    order = jax.random.permutation(own_key, count)
    heavy_load, usual = load_shares(count, rows * top, reach, lean, True), load_shares(count, rows * top, reach, lean, False)
    places = jnp.arange(count)

    def named(sizes, turn):
        used = int((sizes > 0).sum())
        fixed = max(1, used // 4)
        passed = fixed + (places - fixed + turn * (used - fixed)) % max(1, count - fixed)
        return jnp.zeros((count,), jnp.int32).at[order[jnp.where(places < fixed, places, passed)]].set(jnp.asarray(sizes, jnp.int32))

    sizes = jnp.where(number % 4 == 0, named(heavy_load, number // 4), named(usual, number - number // 4 - 1))
    mixed = jax.random.permutation(jax.random.fold_in(own, 3), count)
    source_of, receiver = mixed[0:count // 2 * 2:2], mixed[1:count // 2 * 2:2]
    room = jnp.minimum(sizes[source_of] - 1, reach - sizes[receiver]) // 2
    room = jnp.where((source_of == order[0]) | (receiver == order[0]) | (sizes[receiver] == 0), 0, jnp.maximum(room, 0))
    passed = jax.random.randint(jax.random.fold_in(own, 4), (count // 2,), 0, 1 << 20) % (room + 1)
    sizes = sizes.at[source_of].add(-passed).at[receiver].add(passed)
    labels = jnp.searchsorted(jnp.cumsum(sizes), jnp.arange(rows * top), side="right").astype(jnp.int32)
    table = labels.reshape(top, rows).T
    table = table[jax.random.permutation(jax.random.fold_in(own, 1), rows)]
    turn = jax.random.randint(jax.random.fold_in(own, 2), (rows, 1), 0, top)
    return jnp.take_along_axis(table, (jnp.arange(top)[None, :] + turn) % top, axis=1)


def load_shares(count, total, bound, slope, full):
    loads = [(1 << 20) // math.isqrt(rank ** slope) + 1 for rank in range(1, count + 1)]
    largest = bound if full else min(bound, max(-(-total // count), total * loads[0] // sum(loads)))
    least = 1 if total - largest >= count - 1 else 0
    given, rest = [largest] + [least] * (count - 1), total - largest - least * (count - 1)
    while rest > 0:
        candidates = [i for i in range(1, count) if given[i] < largest] or [i for i in range(1, count) if given[i] < bound]
        pool, budget = sum([loads[i] for i in candidates]), rest
        for i in candidates:
            extra = min(bound - given[i], max(1, budget * loads[i] // pool), rest)
            given[i] = given[i] + extra
            rest = rest - extra
    return np.array(given)


def gaussian(own_key, shape, spread, reach, cuts=(), kind=jnp.bfloat16):
    array = jax.random.normal(own_key, shape, jnp.float32) * spread
    if len(cuts) > 0:
        array = shard_levels(own_key, shape, cuts, -0.22, 0.18) * array
    return jnp.clip(array, min=-reach, max=reach).astype(kind)


def setup_inputs(seed: int = 0) -> dict:
    splits = jax.random.split(jax.random.key(seed), 13)
    tokens = gaussian(splits[0], (TOKENS, D), 1.0, 6.0, ((0, 32),))
    attend_weight = gaussian(splits[1], (D, KHEADS, 2 * DK), D ** -0.5, 0.125, ((1, 4),))
    value_weight = gaussian(splits[2], (D, VHEADS, 2 * DV), D ** -0.5, 0.125, ((1, 4),))
    rate_weight = gaussian(splits[3], (D, VHEADS, 2), D ** -0.5, 0.125, ((1, 4),))
    decay_rate = jnp.clip(jnp.exp(math.log(0.2) - 4.6051702 * jax.random.uniform(splits[4], (VHEADS,), jnp.float32) ** shard_levels(splits[4], (VHEADS,), ((0, 4),), -0.2, 0.2)), 0.002, 0.2)
    output_weight = gaussian(splits[5], (VHEADS, DV, D), (VHEADS * DV) ** -0.5, 0.09375, ((0, 4),))
    state_cache = gaussian(splits[6], (N_REP * TRAJ, VHEADS, DV, DK), 0.3, 2.4, ((0, 8), (1, 4)), jnp.float32)
    resume_from = draw_resume_from(jax.random.fold_in(splits[12], 71), 0)
    expert_index_keys = jax.random.split(jax.random.fold_in(splits[8], 1), TOKENS // ROWS)
    expert_index_turns = jax.random.permutation(jax.random.fold_in(splits[8], 3), TOKENS // ROWS)
    expert_index = jax.vmap(lambda own, number: routed_block(jax.random.fold_in(splits[8], 2), own, number, ROWS, EXPERTS, TOP, ROWS, 2))(expert_index_keys, expert_index_turns).reshape((TOKENS, TOP))
    route_weight = jnp.clip(jnp.exp(math.log(0.3) - 2.7080503 * jax.random.uniform(splits[9], (TOKENS, TOP), jnp.float32) ** shard_levels(splits[9], (TOKENS, TOP), ((0, 32),), -0.2, 0.2)), 0.02, 0.3)
    expert_inner = gaussian(splits[10], (EXPERTS, D, 2 * MI), D ** -0.5, 0.125, ((0, 4),))
    expert_outer = gaussian(splits[11], (EXPERTS, MI, D), MI ** -0.5, 0.25, ((0, 4),))
    return dict(tokens=tokens, attend_weight=attend_weight, value_weight=value_weight, rate_weight=rate_weight, decay_rate=decay_rate, output_weight=output_weight, state_cache=state_cache, resume_from=resume_from, expert_index=expert_index, route_weight=route_weight, expert_inner=expert_inner, expert_outer=expert_outer)


EPSILON = 1e-06
HIGHEST = lax.Precision.HIGHEST

def rms_scale(values):
    return values * lax.rsqrt(lax.optimization_barrier(jnp.mean(values * values, axis=-1, keepdims=True)) + EPSILON)

def unit_length(values):
    return values * lax.rsqrt(lax.optimization_barrier(jnp.sum(values * values, axis=-1, keepdims=True)) + EPSILON)

def head_inputs(attend_part, value_part, rate_part, key_heads, value_heads, decay_rate):
    count = attend_part.shape[0]
    key_size = attend_part.shape[1] // (2 * key_heads)
    value_size = value_part.shape[1] // (2 * value_heads)
    paired = attend_part.reshape(count, key_heads, 2, key_size)
    repeat = value_heads // key_heads
    query = jnp.repeat(unit_length(paired[:, :, 0]), repeat, axis=1) * key_size ** (-0.5)
    key_rows = jnp.repeat(unit_length(paired[:, :, 1]), repeat, axis=1)
    value_pair = value_part.reshape(count, value_heads, 2, value_size)
    rate_pair = rate_part.reshape(count, value_heads, 2)
    beta_rows = jax.nn.sigmoid(rate_pair[:, :, 1])
    log_decay = -decay_rate[None, :] * jax.nn.softplus(rate_pair[:, :, 0])
    return (query, key_rows, value_pair[:, :, 0], value_pair[:, :, 1], beta_rows, log_decay)

def reference(tokens, attend_weight, value_weight, rate_weight, decay_rate, output_weight, state_cache, resume_from, expert_index, route_weight, expert_inner, expert_outer):
    model = tokens.shape[1]
    key_heads = attend_weight.shape[1]
    value_heads = value_weight.shape[1]
    residual = tokens.astype(jnp.float32)
    normed = rms_scale(residual).astype(jnp.bfloat16)
    attend_part = jnp.dot(normed, attend_weight.reshape(model, -1), preferred_element_type=jnp.float32)
    value_part = jnp.dot(normed, value_weight.reshape(model, -1), preferred_element_type=jnp.float32)
    rate_part = jnp.dot(normed, rate_weight.reshape(model, -1), preferred_element_type=jnp.float32)
    query, key_rows, value_rows, gate_rows, beta_rows, log_decay = head_inputs(attend_part, value_part, rate_part, key_heads, value_heads, decay_rate)
    trajectories = N_REP * TRAJ

    def regroup(values):
        return values.reshape((trajectories, LEN) + values.shape[1:])
    start = jnp.take(state_cache, resume_from, axis=0)

    def one_trajectory(packed):
        query_t, key_t, value_t, beta_t, decay_t, state = packed

        def advance(carry, item):
            query_s, key_s, value_s, beta_s, decay_s = item
            carry = jnp.exp(decay_s)[:, None, None] * carry
            predicted = jnp.einsum('hvk,hk->hv', carry, key_s, precision=HIGHEST)
            carry = carry + (beta_s[:, None] * (value_s - predicted))[:, :, None] * key_s[:, None, :]
            return (carry, jnp.einsum('hvk,hk->hv', carry, query_s, precision=HIGHEST))
        return lax.scan(advance, state, (query_t, key_t, value_t, beta_t, decay_t))
    final_state, readout = lax.map(one_trajectory, (regroup(query), regroup(key_rows), regroup(value_rows), regroup(beta_rows), regroup(log_decay), start))
    readout = readout.reshape(value_rows.shape)
    gated = (rms_scale(readout) * jax.nn.silu(gate_rows)).astype(jnp.bfloat16).reshape(readout.shape[0], -1)
    attended = jnp.dot(gated, output_weight.reshape(-1, model), preferred_element_type=jnp.float32)
    hidden = residual + attended
    hidden_normed = rms_scale(hidden).astype(jnp.bfloat16)
    inner = expert_outer.shape[1]

    def add_expert(total, packed):
        inner_matrix, outer_matrix, number = packed
        share = lax.optimization_barrier(jnp.sum(jnp.where(expert_index == number, route_weight, jnp.zeros_like(route_weight)), axis=1))
        both_parts = jnp.dot(hidden_normed, inner_matrix, preferred_element_type=jnp.float32)
        activated = (jax.nn.silu(both_parts[:, :inner]) * both_parts[:, inner:]).astype(jnp.bfloat16)
        produced = jnp.dot(activated, outer_matrix, preferred_element_type=jnp.float32).astype(jnp.bfloat16)
        return (total + share[:, None] * produced.astype(jnp.float32), None)
    numbers = jnp.arange(expert_inner.shape[0], dtype=jnp.int32)
    expert_sum, unused = lax.scan(add_expert, jnp.zeros(hidden.shape, jnp.float32), (expert_inner, expert_outer, numbers))
    layer_output = (hidden + expert_sum).astype(jnp.bfloat16)
    return (layer_output, final_state)
```

```python
import jax
import jax.numpy as jnp
from jax import lax
from jax.experimental import pallas as pl
from jax.experimental.pallas import tpu as pltpu
from jax.sharding import PartitionSpec as P

EPSILON = 1e-06
HIGHEST = lax.Precision.HIGHEST
BF = jnp.bfloat16
F32 = jnp.float32


def rms_scale(values):
    return values * lax.rsqrt(jnp.mean(values * values, axis=-1, keepdims=True) + EPSILON)


def unit_length(values):
    return values * lax.rsqrt(jnp.sum(values * values, axis=-1, keepdims=True) + EPSILON)


def dot_nt(left, right):
    return lax.dot_general(
        left, right, (((1,), (1,)), ((), ())), preferred_element_type=F32
    )


def dot_tn(left, right):
    return lax.dot_general(
        left, right, (((0,), (0,)), ((), ())), preferred_element_type=F32
    )


def dot_nn(left, right):
    return jnp.dot(left, right, preferred_element_type=F32)


def pick_kernel(slot_ref, cache_ref, out_ref):
    out_ref[...] = cache_ref[...].astype(BF)


def pick_states(cache, slots):
    shape = cache.shape
    rows = slots.shape[0]
    block = (1,) + shape[1:]
    return pl.pallas_call(
        pick_kernel,
        grid_spec=pltpu.PrefetchScalarGridSpec(
            num_scalar_prefetch=1,
            grid=(rows,),
            in_specs=[pl.BlockSpec(block, lambda i, slot: (slot[i], 0, 0, 0))],
            out_specs=pl.BlockSpec(block, lambda i, slot: (i, 0, 0, 0)),
        ),
        out_shape=jax.ShapeDtypeStruct((rows,) + shape[1:], BF),
        compiler_params=pltpu.CompilerParams(vmem_limit_bytes=32 << 20),
    )(slots, cache)


def delta_kernel(source_ref, qk_ref, vz_ref, rate_ref, decay_ref, state_ref, gated_ref, final_ref):
    length = qk_ref.shape[0]
    value_heads, size, key_size = state_ref.shape[1:]
    key_heads = qk_ref.shape[1] // (2 * key_size)
    group = value_heads // key_heads
    wide = group * length
    rate = rate_ref[...]
    beta = jax.nn.sigmoid(rate)
    log_decay = -decay_ref[...] * jax.nn.softplus(rate)
    row = lax.broadcasted_iota(jnp.int32, (length, length), 0)
    col = lax.broadcasted_iota(jnp.int32, (length, length), 1)
    lower = (col <= row).astype(F32)
    summed = jnp.dot(lower, log_decay, precision=HIGHEST, preferred_element_type=F32)
    summed_rows = summed.T
    grow = jnp.exp(summed)
    closing = summed[length - 1 : length, :]
    tail = jnp.exp(closing - summed)
    close = jnp.exp(closing)

    wrow = lax.broadcasted_iota(jnp.int32, (wide, wide), 0)
    wcol = lax.broadcasted_iota(jnp.int32, (wide, wide), 1)
    same = wrow // length == wcol // length
    inclusive = same & (wcol <= wrow)
    strict = same & (wcol < wrow)
    eye = (wrow == wcol).astype(F32)

    def stack(values, at):
        return jnp.concatenate(
            [values[:, 2 * h + at : 2 * h + at + 1] for h in at_heads], axis=0
        )

    units = []
    for kh in range(key_heads):
        base = kh * 2 * key_size
        at_heads = range(kh * group, (kh + 1) * group)
        query = (unit_length(qk_ref[:, base : base + key_size]) * key_size ** (-0.5)).astype(BF)
        keys = unit_length(qk_ref[:, base + key_size : base + 2 * key_size]).astype(BF)
        both = jnp.concatenate([query] * group + [keys] * group, axis=0)
        keys_wide = both[wide:]
        products = dot_nt(both, keys_wide)
        states = state_ref[0, kh * group : (kh + 1) * group].reshape(group * size, key_size)
        carried = dot_nt(jnp.concatenate([query, keys], axis=0), states)
        cum_rows = jnp.concatenate([summed_rows[2 * h : 2 * h + 1, :] for h in at_heads], axis=1)
        spread = stack(summed, 0) - cum_rows
        ratio = jnp.where(inclusive, jnp.exp(jnp.minimum(spread, 0.0)), 0.0)
        beta_col = stack(beta, 1)
        grow_col = stack(grow, 0)
        below = jnp.where(strict, beta_col * ratio * products[wide:], 0.0)
        mixing = (ratio * products[:wide]).astype(BF)
        values = jnp.concatenate(
            [vz_ref[:, 2 * h * size : (2 * h + 1) * size] for h in at_heads], axis=0
        ).astype(F32)
        query_part = jnp.concatenate(
            [carried[:length, i * size : (i + 1) * size] for i in range(group)], axis=0
        )
        key_part = jnp.concatenate(
            [carried[length:, i * size : (i + 1) * size] for i in range(group)], axis=0
        )
        right_side = beta_col * (values - grow_col * key_part)
        units.append((keys, below, mixing, right_side, grow_col * query_part))

    inverses = []
    span = 1
    while span < length:
        corner = (wrow // (2 * span) == wcol // (2 * span)) & (
            (wrow // span) % 2 == 1
        ) & ((wcol // span) % 2 == 0)
        corners = [jnp.where(corner, unit[1], 0.0) for unit in units]
        if span == 1:
            inverses = [eye - c for c in corners]
        else:
            rounded = [t.astype(BF) for t in inverses]
            first = [dot_nn(c.astype(BF), t) for c, t in zip(corners, rounded)]
            inverses = [
                t - dot_nn(r, f.astype(BF)) for t, r, f in zip(inverses, rounded, first)
            ]
        span *= 2

    for kh in range(key_heads):
        keys, _, mixing, right_side, read = units[kh]
        updates = dot_nn(inverses[kh].astype(BF), right_side.astype(BF))
        readout = read + dot_nn(mixing, updates.astype(BF))
        scaled = rms_scale(readout)
        tailed = []
        for i in range(group):
            h = kh * group + i
            part = slice(i * length, (i + 1) * length)
            gate = vz_ref[:, (2 * h + 1) * size : (2 * h + 2) * size].astype(F32)
            gated_ref[:, h * size : (h + 1) * size] = (
                scaled[part] * jax.nn.silu(gate)
            ).astype(BF)
            tailed.append(updates[part] * tail[:, 2 * h : 2 * h + 1])
        added = dot_tn(jnp.concatenate(tailed, axis=1).astype(BF), keys)
        for i in range(group):
            h = kh * group + i
            final_ref[0, h] = (
                close[:, 2 * h : 2 * h + 1] * state_ref[0, h].astype(F32)
                + added[i * size : (i + 1) * size]
            )


def delta_rule(source, qk, vz, rate, decay_pairs, states):
    trajs = source.shape[0]
    length = qk.shape[0] // trajs
    heads, size, key_size = states.shape[1:]
    rows = lambda width: pl.BlockSpec((length, width), lambda i, s: (i, 0))
    return pl.pallas_call(
        delta_kernel,
        grid_spec=pltpu.PrefetchScalarGridSpec(
            num_scalar_prefetch=1,
            grid=(trajs,),
            in_specs=[
                rows(qk.shape[1]),
                rows(vz.shape[1]),
                rows(rate.shape[1]),
                pl.BlockSpec((1, rate.shape[1]), lambda i, s: (0, 0)),
                pl.BlockSpec((1, heads, size, key_size), lambda i, s: (s[i], 0, 0, 0)),
            ],
            out_specs=[
                rows(heads * size),
                pl.BlockSpec((1, heads, size, key_size), lambda i, s: (i, 0, 0, 0)),
            ],
        ),
        out_shape=[
            jax.ShapeDtypeStruct((qk.shape[0], heads * size), BF),
            jax.ShapeDtypeStruct((trajs, heads, size, key_size), F32),
        ],
        compiler_params=pltpu.CompilerParams(vmem_limit_bytes=48 << 20),
    )(source, qk, vz, rate, decay_pairs, states)


def local(
    tokens,
    attend_weight,
    value_weight,
    rate_weight,
    decay_rate,
    output_weight,
    state_cache,
    resume_from,
    expert_index,
    route_weight,
    expert_inner,
    expert_outer,
):
    model = tokens.shape[1]
    value_heads = value_weight.shape[1]
    residual = tokens.astype(F32)
    normed = rms_scale(residual).astype(BF)
    piece = lax.all_gather(normed, "exp", axis=0, tiled=True)

    trajs = state_cache.shape[0]
    replicas = lax.axis_size("rep")
    myself = lax.axis_index("rep")
    my_rows = lax.dynamic_slice_in_dim(resume_from, myself * trajs, trajs)
    listing = resume_from.reshape(replicas, trajs)
    from_me = listing // trajs == myself
    slot_pick = jnp.sum(jnp.where(from_me, listing % trajs, 0), axis=1)
    outgoing = pick_states(state_cache, slot_pick)
    incoming = lax.all_to_all(outgoing, "rep", split_axis=0, concat_axis=0, tiled=True)

    local_experts = expert_inner.shape[0]
    total_experts = lax.axis_size("exp") * local_experts
    numbers = jnp.arange(total_experts, dtype=jnp.int32)
    share = jnp.sum(
        jnp.where(expert_index[None] == numbers[:, None, None], route_weight[None], 0.0), axis=2
    )
    shares = lax.all_to_all(
        share.reshape(lax.axis_size("exp"), local_experts, -1),
        "exp", split_axis=0, concat_axis=0, tiled=True,
    )
    shares = jnp.moveaxis(shares, 1, 0).reshape(local_experts, -1)

    qk = jnp.dot(piece, attend_weight.reshape(model, -1), preferred_element_type=F32)
    vz = jnp.dot(piece, value_weight.reshape(model, -1), preferred_element_type=F32).astype(BF)
    rate = jnp.dot(piece, rate_weight.reshape(model, -1), preferred_element_type=F32)
    decay_pairs = jnp.repeat(decay_rate, 2)[None, :]
    gated, final_state = delta_rule(my_rows // trajs, qk, vz, rate, decay_pairs, incoming)

    output_flat = output_weight.reshape(-1, model)
    attended = lax.psum_scatter(
        jnp.dot(gated, output_flat, preferred_element_type=F32).astype(BF),
        "exp",
        scatter_dimension=0,
        tiled=True,
    ).astype(F32)
    hidden = residual + attended
    hidden_normed = rms_scale(hidden).astype(BF)
    everyone = lax.all_gather(hidden_normed, "exp", axis=0, tiled=True)
    inner = expert_outer.shape[1]
    weighted = 0.0
    for e in range(local_experts):
        both_parts = jnp.dot(everyone, expert_inner[e], preferred_element_type=F32)
        activated = (jax.nn.silu(both_parts[:, :inner]) * both_parts[:, inner:]).astype(BF)
        produced = jnp.dot(activated, expert_outer[e], preferred_element_type=F32)
        weighted = weighted + shares[e][:, None] * produced
    expert_sum = lax.psum_scatter(
        weighted.astype(BF), "exp", scatter_dimension=0, tiled=True
    ).astype(F32)
    layer_output = (hidden + expert_sum).astype(BF)
    return (layer_output, final_state)


def solution(mesh):
    in_specs = (
        P(("rep", "exp"), None),
        P(None, "exp", None),
        P(None, "exp", None),
        P(None, "exp", None),
        P("exp"),
        P("exp", None, None),
        P("rep", "exp", None, None),
        P(),
        P(("rep", "exp"), None),
        P(("rep", "exp"), None),
        P("exp", None, None),
        P("exp", None, None),
    )
    out_specs = (P(("rep", "exp"), None), P("rep", "exp", None, None))
    return jax.shard_map(local, mesh=mesh, in_specs=in_specs, out_specs=out_specs, check_vma=False)
```

```python
from functools import partial

import jax
import jax.numpy as jnp
from jax import lax
from jax.experimental import pallas as pl
from jax.experimental.pallas import tpu as pltpu
from jax.sharding import PartitionSpec as P

EPSILON = 1e-06
HIGHEST = lax.Precision.HIGHEST
BF = jnp.bfloat16
F32 = jnp.float32


def rms_scale(values):
    return values * lax.rsqrt(jnp.mean(values * values, axis=-1, keepdims=True) + EPSILON)


def unit_length(values):
    return values * lax.rsqrt(jnp.sum(values * values, axis=-1, keepdims=True) + EPSILON)


def dot_nt(left, right):
    return lax.dot_general(
        left, right, (((1,), (1,)), ((), ())), preferred_element_type=F32
    )


def dot_tn(left, right):
    return lax.dot_general(
        left, right, (((0,), (0,)), ((), ())), preferred_element_type=F32
    )


def dot_nn(left, right):
    return jnp.dot(left, right, preferred_element_type=F32)


def pick_kernel(slot_ref, cache_ref, out_ref):
    out_ref[...] = cache_ref[...].astype(BF)


def pick_states(cache, slots):
    shape = cache.shape
    rows = slots.shape[0]
    block = (1,) + shape[1:]
    return pl.pallas_call(
        pick_kernel,
        grid_spec=pltpu.PrefetchScalarGridSpec(
            num_scalar_prefetch=1,
            grid=(rows,),
            in_specs=[pl.BlockSpec(block, lambda i, slot: (slot[i], 0, 0, 0))],
            out_specs=pl.BlockSpec(block, lambda i, slot: (i, 0, 0, 0)),
        ),
        out_shape=jax.ShapeDtypeStruct((rows,) + shape[1:], BF),
        compiler_params=pltpu.CompilerParams(vmem_limit_bytes=32 << 20),
    )(slots, cache)


def solve_kernel(qk_ref, rate_ref, decay_ref, unit_ref, inverse_ref, mixing_ref, coef_ref):
    length = qk_ref.shape[0]
    wide = inverse_ref.shape[-1]
    group = wide // length
    key_heads = inverse_ref.shape[1]
    key_size = qk_ref.shape[1] // (2 * key_heads)
    rate = rate_ref[...]
    beta = jax.nn.sigmoid(rate)
    log_decay = -decay_ref[...] * jax.nn.softplus(rate)
    row = lax.broadcasted_iota(jnp.int32, (length, length), 0)
    col = lax.broadcasted_iota(jnp.int32, (length, length), 1)
    lower = (col <= row).astype(F32)
    summed = jnp.dot(lower, log_decay, precision=HIGHEST, preferred_element_type=F32)
    summed_rows = summed.T
    closing = summed[length - 1 : length, :]
    coef_ref[...] = jnp.concatenate(
        [
            beta,
            jnp.exp(summed),
            jnp.exp(closing - summed),
            jnp.broadcast_to(jnp.exp(closing), summed.shape),
        ],
        axis=1,
    )

    wrow = lax.broadcasted_iota(jnp.int32, (wide, wide), 0)
    wcol = lax.broadcasted_iota(jnp.int32, (wide, wide), 1)
    same = wrow // length == wcol // length
    inclusive = same & (wcol <= wrow)
    strict = same & (wcol < wrow)
    eye = (wrow == wcol).astype(F32)

    belows = []
    for kh in range(key_heads):
        base = kh * 2 * key_size
        heads = range(kh * group, (kh + 1) * group)
        query = (unit_length(qk_ref[:, base : base + key_size]) * key_size ** (-0.5)).astype(BF)
        keys = unit_length(qk_ref[:, base + key_size : base + 2 * key_size]).astype(BF)
        unit_ref[0, kh] = jnp.concatenate([query, keys], axis=0)
        both = jnp.concatenate([query] * group + [keys] * group, axis=0)
        products = dot_nt(both, both[wide:])
        sum_col = jnp.concatenate([summed[:, 2 * h : 2 * h + 1] for h in heads], axis=0)
        sum_row = jnp.concatenate([summed_rows[2 * h : 2 * h + 1, :] for h in heads], axis=1)
        beta_col = jnp.concatenate([beta[:, 2 * h + 1 : 2 * h + 2] for h in heads], axis=0)
        spread = sum_col - sum_row
        ratio = jnp.where(inclusive, jnp.exp(jnp.minimum(spread, 0.0)), 0.0)
        belows.append(jnp.where(strict, beta_col * ratio * products[wide:], 0.0))
        mixing_ref[0, kh] = (ratio * products[:wide]).astype(BF)

    span = 1
    inverses = []
    while span < length:
        corner = (wrow // (2 * span) == wcol // (2 * span)) & (
            (wrow // span) % 2 == 1
        ) & ((wcol // span) % 2 == 0)
        corners = [jnp.where(corner, below, 0.0) for below in belows]
        if span == 1:
            inverses = [eye - c for c in corners]
        else:
            rounded = [t.astype(BF) for t in inverses]
            first = [dot_nn(c.astype(BF), t) for c, t in zip(corners, rounded)]
            inverses = [
                t - dot_nn(r, f.astype(BF)) for t, r, f in zip(inverses, rounded, first)
            ]
        span *= 2
    for kh in range(key_heads):
        inverse_ref[0, kh] = inverses[kh].astype(BF)


def state_kernel(
    source_ref, vz_ref, unit_ref, inverse_ref, mixing_ref, coef_ref, state_ref, gated_ref, final_ref
):
    length = vz_ref.shape[0]
    value_heads, size, key_size = state_ref.shape[1:]
    key_heads = inverse_ref.shape[1]
    group = value_heads // key_heads
    pairs = coef_ref.shape[1] // 4
    coef = coef_ref[...]

    def column(kind, h, at=0):
        place = kind * pairs + 2 * h + at
        return coef[:, place : place + 1]

    def stack(parts):
        return jnp.concatenate(list(parts), axis=0)

    carrieds = []
    for kh in range(key_heads):
        states = state_ref[0, kh * group : (kh + 1) * group].reshape(group * size, key_size)
        carrieds.append(dot_nt(unit_ref[0, kh], states))
    updates = []
    for kh in range(key_heads):
        heads = range(kh * group, (kh + 1) * group)
        beta_col = stack(column(0, h, 1) for h in heads)
        grow_col = stack(column(1, h) for h in heads)
        values = stack(vz_ref[:, 2 * h * size : (2 * h + 1) * size] for h in heads).astype(F32)
        key_part = stack(
            carrieds[kh][length:, i * size : (i + 1) * size] for i in range(group)
        )
        right_side = beta_col * (values - grow_col * key_part)
        updates.append(dot_nn(inverse_ref[0, kh], right_side.astype(BF)))
    readouts = []
    addeds = []
    for kh in range(key_heads):
        heads = range(kh * group, (kh + 1) * group)
        grow_col = stack(column(1, h) for h in heads)
        query_part = stack(
            carrieds[kh][:length, i * size : (i + 1) * size] for i in range(group)
        )
        readouts.append(
            grow_col * query_part + dot_nn(mixing_ref[0, kh], updates[kh].astype(BF))
        )
        tailed = [
            updates[kh][i * length : (i + 1) * length] * column(2, kh * group + i)
            for i in range(group)
        ]
        addeds.append(
            dot_tn(jnp.concatenate(tailed, axis=1).astype(BF), unit_ref[0, kh][length:])
        )
    for kh in range(key_heads):
        scaled = rms_scale(readouts[kh])
        for i in range(group):
            h = kh * group + i
            gate = vz_ref[:, (2 * h + 1) * size : (2 * h + 2) * size].astype(F32)
            gated_ref[:, h * size : (h + 1) * size] = (
                scaled[i * length : (i + 1) * length] * jax.nn.silu(gate)
            ).astype(BF)
            final_ref[0, h] = (
                column(3, h)[:1] * state_ref[0, h].astype(F32)
                + addeds[kh][i * size : (i + 1) * size]
            )


def solve_chunks(trajs, key_heads, value_heads, qk, rate, decay_pairs):
    length = qk.shape[0] // trajs
    wide = length * (value_heads // key_heads)
    key_size = qk.shape[1] // (2 * key_heads)
    rows = lambda width: pl.BlockSpec((length, width), lambda i: (i, 0))
    heads = lambda a, b: pl.BlockSpec((1, key_heads, a, b), lambda i: (i, 0, 0, 0))
    return pl.pallas_call(
        solve_kernel,
        grid=(trajs,),
        in_specs=[
            rows(qk.shape[1]),
            rows(rate.shape[1]),
            pl.BlockSpec((1, rate.shape[1]), lambda i: (0, 0)),
        ],
        out_specs=[
            heads(2 * length, key_size),
            heads(wide, wide),
            heads(wide, wide),
            rows(4 * rate.shape[1]),
        ],
        out_shape=[
            jax.ShapeDtypeStruct((trajs, key_heads, 2 * length, key_size), BF),
            jax.ShapeDtypeStruct((trajs, key_heads, wide, wide), BF),
            jax.ShapeDtypeStruct((trajs, key_heads, wide, wide), BF),
            jax.ShapeDtypeStruct((qk.shape[0], 4 * rate.shape[1]), F32),
        ],
        compiler_params=pltpu.CompilerParams(vmem_limit_bytes=32 << 20),
        cost_estimate=pl.CostEstimate(
            flops=trajs * key_heads * 26 * wide**3, bytes_accessed=6 << 20, transcendentals=0
        ),
    )(qk, rate, decay_pairs)


def apply_states(source, vz, unit, inverse, mixing, coef, states):
    trajs = source.shape[0]
    length = vz.shape[0] // trajs
    heads, size, key_size = states.shape[1:]
    rows = lambda width: pl.BlockSpec((length, width), lambda i, s: (i, 0))
    whole = lambda array: pl.BlockSpec((1,) + array.shape[1:], lambda i, s: (i, 0, 0, 0))
    return pl.pallas_call(
        state_kernel,
        grid_spec=pltpu.PrefetchScalarGridSpec(
            num_scalar_prefetch=1,
            grid=(trajs,),
            in_specs=[
                rows(vz.shape[1]),
                whole(unit),
                whole(inverse),
                whole(mixing),
                rows(coef.shape[1]),
                pl.BlockSpec((1, heads, size, key_size), lambda i, s: (s[i], 0, 0, 0)),
            ],
            out_specs=[
                rows(heads * size),
                pl.BlockSpec((1, heads, size, key_size), lambda i, s: (i, 0, 0, 0)),
            ],
        ),
        out_shape=[
            jax.ShapeDtypeStruct((vz.shape[0], heads * size), BF),
            jax.ShapeDtypeStruct((trajs, heads, size, key_size), F32),
        ],
        compiler_params=pltpu.CompilerParams(vmem_limit_bytes=32 << 20),
        cost_estimate=pl.CostEstimate(
            flops=trajs * heads * 8 * length * size * size, bytes_accessed=10 << 20, transcendentals=0
        ),
    )(source, vz, unit, inverse, mixing, coef, states)


def chunk_rows(rows):
    return max(16, rows // 4)


def enter(me, chips):
    core = me % 2
    barrier = pltpu.get_barrier_semaphore()
    pl.semaphore_signal(barrier, inc=1, device_id={"exp": me + 1 - 2 * core})
    for j in range(1, chips):
        mate = lax.rem(me // 2 + j, chips) * 2 + core
        pl.semaphore_signal(barrier, inc=1, device_id={"exp": mate})
    pl.semaphore_wait(barrier, chips)


def summed_chunks(me, chips, part_ref, near_ref, out_ref, far_ref, sems, finish):
    near_send, near_recv, far_send, far_recv = sems
    core, chip = me % 2, me // 2
    sibling = me + 1 - 2 * core
    rows = near_ref.shape[1]
    step = chunk_rows(rows)
    count = rows // step
    order = [(j, k) for j in list(range(1, chips)) + [0] for k in range(count)]

    def block(j, which, k):
        start = (lax.rem(chip + j, chips) * 2 + which) * rows + k * step
        return pl.ds(pl.multiple_of(start, step), step)

    near, far = {}, {}
    for j, k in order:
        near[j, k] = pltpu.make_async_remote_copy(
            src_ref=part_ref.at[block(j, 1 - core, k)],
            dst_ref=near_ref.at[j, pl.ds(k * step, step)],
            send_sem=near_send.at[j * count + k],
            recv_sem=near_recv.at[j * count + k],
            device_id={"exp": sibling},
        )
        near[j, k].start()
    for j, k in order:
        if j == 0:
            continue
        here = pl.ds(k * step, step)
        near[j, k].wait_recv()
        out_ref[j, here] = (
            part_ref[block(j, core, k)].astype(F32) + near_ref[j, here].astype(F32)
        ).astype(BF)
        far[j, k] = pltpu.make_async_remote_copy(
            src_ref=out_ref.at[j, here],
            dst_ref=far_ref.at[j, here],
            send_sem=far_send.at[j * count + k],
            recv_sem=far_recv.at[j * count + k],
            device_id={"exp": lax.rem(chip + j, chips) * 2 + core},
        )
        far[j, k].start()
    for k in range(count):
        here = pl.ds(k * step, step)
        near[0, k].wait_recv()
        total = part_ref[block(0, core, k)].astype(F32) + near_ref[0, here].astype(F32)
        for j in range(1, chips):
            far[j, k].wait_recv()
            total = total + far_ref[j, here].astype(F32)
        finish(k, here, total)
    return list(near.values()) + list(far.values())


def spread_kernel(
    chips, part_ref, tokens_ref, every_ref, hidden_ref, near_ref, out_ref, far_ref,
    near_send, near_recv, far_send, far_recv, share_send, share_recv, cross_send, cross_recv,
):
    me = lax.axis_index("exp")
    core, chip = me % 2, me // 2
    sibling = me + 1 - 2 * core
    rows = tokens_ref.shape[0]
    step = chunk_rows(rows)
    count = rows // step
    enter(me, chips)
    share, cross = {}, {}

    def place(owner, k):
        return pl.ds(pl.multiple_of(owner * rows + k * step, step), step)

    def send(where, j, k, device, send_sem, recv_sem):
        copy = pltpu.make_async_remote_copy(
            src_ref=every_ref.at[where],
            dst_ref=every_ref.at[where],
            send_sem=send_sem.at[j * count + k],
            recv_sem=recv_sem.at[j * count + k],
            device_id={"exp": device},
        )
        copy.start()
        return copy

    def finish(k, here, total):
        hidden = tokens_ref[here].astype(F32) + total
        hidden_ref[here] = hidden
        mine = place(me, k)
        every_ref[mine] = rms_scale(hidden).astype(BF)
        for j in range(1, chips):
            mate = lax.rem(chip + j, chips) * 2 + core
            cross[j, k] = send(mine, j, k, mate, cross_send, cross_recv)
        share[0, k] = send(mine, 0, k, sibling, share_send, share_recv)

    sems = (near_send, near_recv, far_send, far_recv)
    sent = summed_chunks(me, chips, part_ref, near_ref, out_ref, far_ref, sems, finish)
    for k in range(count):
        for j in range(1, chips):
            cross[j, k].wait_recv()
            owner = lax.rem(chip + chips - j, chips) * 2 + core
            share[j, k] = send(place(owner, k), j, k, sibling, share_send, share_recv)
    for copy in share.values():
        copy.wait_recv()
    for copy in sent + list(share.values()) + list(cross.values()):
        copy.wait_send()


def final_kernel(
    chips, part_ref, hidden_ref, result_ref, near_ref, out_ref, far_ref,
    near_send, near_recv, far_send, far_recv,
):
    me = lax.axis_index("exp")
    enter(me, chips)

    def finish(k, here, total):
        result_ref[here] = (hidden_ref[here] + total).astype(BF)

    sems = (near_send, near_recv, far_send, far_recv)
    sent = summed_chunks(me, chips, part_ref, near_ref, out_ref, far_ref, sems, finish)
    for copy in sent:
        copy.wait_send()


def remote_call(kernel, chips, collective_id, groups, out_shape, part, own):
    rows, model = own.shape
    copies = chips * (rows // chunk_rows(rows))
    vmem = pl.BlockSpec(memory_space=pltpu.VMEM)
    return pl.pallas_call(
        partial(kernel, chips),
        in_specs=[vmem, vmem],
        out_specs=jax.tree.map(lambda _: vmem, out_shape),
        out_shape=out_shape,
        scratch_shapes=[pltpu.VMEM((chips, rows, model), BF)] * 3
        + [pltpu.SemaphoreType.DMA((copies,))] * (2 * groups),
        compiler_params=pltpu.CompilerParams(
            collective_id=collective_id, has_side_effects=True, vmem_limit_bytes=48 << 20
        ),
    )(part, own)


def local(
    tokens,
    attend_weight,
    value_weight,
    rate_weight,
    decay_rate,
    output_weight,
    state_cache,
    resume_from,
    expert_index,
    route_weight,
    expert_inner,
    expert_outer,
):
    model = tokens.shape[1]
    value_heads = value_weight.shape[1]
    residual = tokens.astype(F32)
    normed = rms_scale(residual).astype(BF)
    piece = lax.all_gather(normed, "exp", axis=0, tiled=True)

    trajs = state_cache.shape[0]
    replicas = lax.axis_size("rep")
    myself = lax.axis_index("rep")
    my_rows = lax.dynamic_slice_in_dim(resume_from, myself * trajs, trajs)
    listing = resume_from.reshape(replicas, trajs)
    from_me = listing // trajs == myself
    slot_pick = jnp.sum(jnp.where(from_me, listing % trajs, 0), axis=1)
    outgoing = pick_states(state_cache, slot_pick)
    incoming = lax.all_to_all(outgoing, "rep", split_axis=0, concat_axis=0, tiled=True)

    local_experts = expert_inner.shape[0]
    total_experts = lax.axis_size("exp") * local_experts
    numbers = jnp.arange(total_experts, dtype=jnp.int32)
    share = jnp.sum(
        jnp.where(expert_index[None] == numbers[:, None, None], route_weight[None], 0.0), axis=2
    )
    shares = lax.all_to_all(
        share.reshape(lax.axis_size("exp"), local_experts, -1),
        "exp", split_axis=0, concat_axis=0, tiled=True,
    )
    shares = jnp.moveaxis(shares, 1, 0).reshape(local_experts, -1)

    qk = jnp.dot(piece, attend_weight.reshape(model, -1), preferred_element_type=F32)
    vz = jnp.dot(piece, value_weight.reshape(model, -1), preferred_element_type=F32).astype(BF)
    rate = jnp.dot(piece, rate_weight.reshape(model, -1), preferred_element_type=F32)
    decay_pairs = jnp.repeat(decay_rate, 2)[None, :]
    solved = solve_chunks(trajs, attend_weight.shape[1], value_heads, qk, rate, decay_pairs)
    gated, final_state = apply_states(my_rows // trajs, vz, *solved, incoming)

    output_flat = output_weight.reshape(-1, model)
    partial_rows = jnp.dot(gated, output_flat, preferred_element_type=F32).astype(BF)
    chips = lax.axis_size("exp") // 2
    everyone, hidden = remote_call(
        spread_kernel,
        chips,
        0,
        4,
        [
            jax.ShapeDtypeStruct(partial_rows.shape, BF),
            jax.ShapeDtypeStruct(tokens.shape, F32),
        ],
        partial_rows,
        tokens,
    )
    inner = expert_outer.shape[1]
    weighted = 0.0
    for e in range(local_experts):
        both_parts = jnp.dot(everyone, expert_inner[e], preferred_element_type=F32)
        activated = (jax.nn.silu(both_parts[:, :inner]) * both_parts[:, inner:]).astype(BF)
        produced = jnp.dot(activated, expert_outer[e], preferred_element_type=F32)
        weighted = weighted + shares[e][:, None] * produced
    layer_output = remote_call(
        final_kernel,
        chips,
        1,
        2,
        jax.ShapeDtypeStruct(tokens.shape, BF),
        weighted.astype(BF),
        hidden,
    )
    return (layer_output, final_state)


def solution(mesh):
    in_specs = (
        P(("rep", "exp"), None),
        P(None, "exp", None),
        P(None, "exp", None),
        P(None, "exp", None),
        P("exp"),
        P("exp", None, None),
        P("rep", "exp", None, None),
        P(),
        P(("rep", "exp"), None),
        P(("rep", "exp"), None),
        P("exp", None, None),
        P("exp", None, None),
    )
    out_specs = (P(("rep", "exp"), None), P("rep", "exp", None, None))
    return jax.shard_map(local, mesh=mesh, in_specs=in_specs, out_specs=out_specs, check_vma=False)
```

```python
from functools import partial

import jax
import jax.numpy as jnp
from jax import lax
from jax.experimental import pallas as pl
from jax.experimental.pallas import tpu as pltpu
from jax.sharding import PartitionSpec as P

EPSILON = 1e-06
HIGHEST = lax.Precision.HIGHEST
BF = jnp.bfloat16
F32 = jnp.float32


def rms_scale(values):
    return values * lax.rsqrt(jnp.mean(values * values, axis=-1, keepdims=True) + EPSILON)


def unit_length(values):
    return values * lax.rsqrt(jnp.sum(values * values, axis=-1, keepdims=True) + EPSILON)


def dot_nt(left, right):
    return lax.dot_general(
        left, right, (((1,), (1,)), ((), ())), preferred_element_type=F32
    )


def dot_tn(left, right):
    return lax.dot_general(
        left, right, (((0,), (0,)), ((), ())), preferred_element_type=F32
    )


def dot_nn(left, right):
    return jnp.dot(left, right, preferred_element_type=F32)


def pick_kernel(slot_ref, cache_ref, out_ref):
    out_ref[...] = cache_ref[...].astype(BF)


def pick_states(cache, slots):
    shape = cache.shape
    rows = slots.shape[0]
    block = (1,) + shape[1:]
    return pl.pallas_call(
        pick_kernel,
        grid_spec=pltpu.PrefetchScalarGridSpec(
            num_scalar_prefetch=1,
            grid=(rows,),
            in_specs=[pl.BlockSpec(block, lambda i, slot: (slot[i], 0, 0, 0))],
            out_specs=pl.BlockSpec(block, lambda i, slot: (i, 0, 0, 0)),
        ),
        out_shape=jax.ShapeDtypeStruct((rows,) + shape[1:], BF),
        compiler_params=pltpu.CompilerParams(vmem_limit_bytes=32 << 20),
    )(slots, cache)


def solve_kernel(qk_ref, rate_ref, decay_ref, unit_ref, inverse_ref, mixing_ref, coef_ref):
    length = qk_ref.shape[0]
    wide = inverse_ref.shape[-1]
    group = wide // length
    key_heads = inverse_ref.shape[1]
    key_size = qk_ref.shape[1] // (2 * key_heads)
    rate = rate_ref[...]
    beta = jax.nn.sigmoid(rate)
    log_decay = -decay_ref[...] * jax.nn.softplus(rate)
    row = lax.broadcasted_iota(jnp.int32, (length, length), 0)
    col = lax.broadcasted_iota(jnp.int32, (length, length), 1)
    lower = (col <= row).astype(F32)
    summed = jnp.dot(lower, log_decay, precision=HIGHEST, preferred_element_type=F32)
    summed_rows = summed.T
    closing = summed[length - 1 : length, :]
    coef_ref[...] = jnp.concatenate(
        [
            beta,
            jnp.exp(summed),
            jnp.exp(closing - summed),
            jnp.broadcast_to(jnp.exp(closing), summed.shape),
        ],
        axis=1,
    )

    wrow = lax.broadcasted_iota(jnp.int32, (wide, wide), 0)
    wcol = lax.broadcasted_iota(jnp.int32, (wide, wide), 1)
    same = wrow // length == wcol // length
    inclusive = same & (wcol <= wrow)
    strict = same & (wcol < wrow)
    eye = (wrow == wcol).astype(F32)

    belows = []
    for kh in range(key_heads):
        base = kh * 2 * key_size
        heads = range(kh * group, (kh + 1) * group)
        query = (unit_length(qk_ref[:, base : base + key_size]) * key_size ** (-0.5)).astype(BF)
        keys = unit_length(qk_ref[:, base + key_size : base + 2 * key_size]).astype(BF)
        unit_ref[0, kh] = jnp.concatenate([query, keys], axis=0)
        both = jnp.concatenate([query] * group + [keys] * group, axis=0)
        products = dot_nt(both, both[wide:])
        sum_col = jnp.concatenate([summed[:, 2 * h : 2 * h + 1] for h in heads], axis=0)
        sum_row = jnp.concatenate([summed_rows[2 * h : 2 * h + 1, :] for h in heads], axis=1)
        beta_col = jnp.concatenate([beta[:, 2 * h + 1 : 2 * h + 2] for h in heads], axis=0)
        spread = sum_col - sum_row
        ratio = jnp.where(inclusive, jnp.exp(jnp.minimum(spread, 0.0)), 0.0)
        belows.append(jnp.where(strict, beta_col * ratio * products[wide:], 0.0))
        mixing_ref[0, kh] = (ratio * products[:wide]).astype(BF)

    span = 1
    inverses = []
    while span < length:
        corner = (wrow // (2 * span) == wcol // (2 * span)) & (
            (wrow // span) % 2 == 1
        ) & ((wcol // span) % 2 == 0)
        corners = [jnp.where(corner, below, 0.0) for below in belows]
        if span == 1:
            inverses = [eye - c for c in corners]
        else:
            rounded = [t.astype(BF) for t in inverses]
            first = [dot_nn(c.astype(BF), t) for c, t in zip(corners, rounded)]
            inverses = [
                t - dot_nn(r, f.astype(BF)) for t, r, f in zip(inverses, rounded, first)
            ]
        span *= 2
    for kh in range(key_heads):
        inverse_ref[0, kh] = inverses[kh].astype(BF)


def state_kernel(
    source_ref, vz_ref, unit_ref, inverse_ref, mixing_ref, coef_ref, state_ref, gated_ref, final_ref
):
    length = vz_ref.shape[0]
    value_heads, size, key_size = state_ref.shape[1:]
    key_heads = inverse_ref.shape[1]
    group = value_heads // key_heads
    pairs = coef_ref.shape[1] // 4
    coef = coef_ref[...]

    def column(kind, h, at=0):
        place = kind * pairs + 2 * h + at
        return coef[:, place : place + 1]

    def stack(parts):
        return jnp.concatenate(list(parts), axis=0)

    carrieds = []
    for kh in range(key_heads):
        states = state_ref[0, kh * group : (kh + 1) * group].reshape(group * size, key_size)
        carrieds.append(dot_nt(unit_ref[0, kh], states))
    updates = []
    for kh in range(key_heads):
        heads = range(kh * group, (kh + 1) * group)
        beta_col = stack(column(0, h, 1) for h in heads)
        grow_col = stack(column(1, h) for h in heads)
        values = stack(vz_ref[:, 2 * h * size : (2 * h + 1) * size] for h in heads).astype(F32)
        key_part = stack(
            carrieds[kh][length:, i * size : (i + 1) * size] for i in range(group)
        )
        right_side = beta_col * (values - grow_col * key_part)
        updates.append(dot_nn(inverse_ref[0, kh], right_side.astype(BF)))
    readouts = []
    addeds = []
    for kh in range(key_heads):
        heads = range(kh * group, (kh + 1) * group)
        grow_col = stack(column(1, h) for h in heads)
        query_part = stack(
            carrieds[kh][:length, i * size : (i + 1) * size] for i in range(group)
        )
        readouts.append(
            grow_col * query_part + dot_nn(mixing_ref[0, kh], updates[kh].astype(BF))
        )
        tailed = [
            updates[kh][i * length : (i + 1) * length] * column(2, kh * group + i)
            for i in range(group)
        ]
        addeds.append(
            dot_tn(jnp.concatenate(tailed, axis=1).astype(BF), unit_ref[0, kh][length:])
        )
    for kh in range(key_heads):
        scaled = rms_scale(readouts[kh])
        for i in range(group):
            h = kh * group + i
            gate = vz_ref[:, (2 * h + 1) * size : (2 * h + 2) * size].astype(F32)
            gated_ref[:, h * size : (h + 1) * size] = (
                scaled[i * length : (i + 1) * length] * jax.nn.silu(gate)
            ).astype(BF)
            final_ref[0, h] = (
                column(3, h)[:1] * state_ref[0, h].astype(F32)
                + addeds[kh][i * size : (i + 1) * size]
            )


def solve_chunks(trajs, key_heads, value_heads, qk, rate, decay_pairs):
    length = qk.shape[0] // trajs
    wide = length * (value_heads // key_heads)
    key_size = qk.shape[1] // (2 * key_heads)
    rows = lambda width: pl.BlockSpec((length, width), lambda i: (i, 0))
    heads = lambda a, b: pl.BlockSpec((1, key_heads, a, b), lambda i: (i, 0, 0, 0))
    return pl.pallas_call(
        solve_kernel,
        grid=(trajs,),
        in_specs=[
            rows(qk.shape[1]),
            rows(rate.shape[1]),
            pl.BlockSpec((1, rate.shape[1]), lambda i: (0, 0)),
        ],
        out_specs=[
            heads(2 * length, key_size),
            heads(wide, wide),
            heads(wide, wide),
            rows(4 * rate.shape[1]),
        ],
        out_shape=[
            jax.ShapeDtypeStruct((trajs, key_heads, 2 * length, key_size), BF),
            jax.ShapeDtypeStruct((trajs, key_heads, wide, wide), BF),
            jax.ShapeDtypeStruct((trajs, key_heads, wide, wide), BF),
            jax.ShapeDtypeStruct((qk.shape[0], 4 * rate.shape[1]), F32),
        ],
        compiler_params=pltpu.CompilerParams(vmem_limit_bytes=32 << 20),
        cost_estimate=pl.CostEstimate(
            flops=trajs * key_heads * 26 * wide**3, bytes_accessed=6 << 20, transcendentals=0
        ),
    )(qk, rate, decay_pairs)


def apply_states(source, vz, unit, inverse, mixing, coef, states):
    trajs = source.shape[0]
    length = vz.shape[0] // trajs
    heads, size, key_size = states.shape[1:]
    rows = lambda width: pl.BlockSpec((length, width), lambda i, s: (i, 0))
    whole = lambda array: pl.BlockSpec((1,) + array.shape[1:], lambda i, s: (i, 0, 0, 0))
    return pl.pallas_call(
        state_kernel,
        grid_spec=pltpu.PrefetchScalarGridSpec(
            num_scalar_prefetch=1,
            grid=(trajs,),
            in_specs=[
                rows(vz.shape[1]),
                whole(unit),
                whole(inverse),
                whole(mixing),
                rows(coef.shape[1]),
                pl.BlockSpec((1, heads, size, key_size), lambda i, s: (s[i], 0, 0, 0)),
            ],
            out_specs=[
                rows(heads * size),
                pl.BlockSpec((1, heads, size, key_size), lambda i, s: (i, 0, 0, 0)),
            ],
        ),
        out_shape=[
            jax.ShapeDtypeStruct((vz.shape[0], heads * size), BF),
            jax.ShapeDtypeStruct((trajs, heads, size, key_size), F32),
        ],
        compiler_params=pltpu.CompilerParams(vmem_limit_bytes=32 << 20),
        cost_estimate=pl.CostEstimate(
            flops=trajs * heads * 8 * length * size * size, bytes_accessed=10 << 20, transcendentals=0
        ),
    )(source, vz, unit, inverse, mixing, coef, states)


def chunk_rows(rows):
    return max(16, rows // 4)


def enter(me, chips):
    core = me % 2
    barrier = pltpu.get_barrier_semaphore()
    pl.semaphore_signal(barrier, inc=1, device_id={"exp": me + 1 - 2 * core})
    for j in range(1, chips):
        mate = lax.rem(me // 2 + j, chips) * 2 + core
        pl.semaphore_signal(barrier, inc=1, device_id={"exp": mate})
    pl.semaphore_wait(barrier, chips)


def summed_chunks(me, chips, part_ref, near_ref, out_ref, far_ref, sems, finish):
    near_send, near_recv, far_send, far_recv = sems
    core, chip = me % 2, me // 2
    sibling = me + 1 - 2 * core
    rows = near_ref.shape[1]
    step = chunk_rows(rows)
    count = rows // step
    order = [(j, k) for j in list(range(1, chips)) + [0] for k in range(count)]

    def block(j, which, k):
        start = (lax.rem(chip + j, chips) * 2 + which) * rows + k * step
        return pl.ds(pl.multiple_of(start, step), step)

    near, far = {}, {}
    for j, k in order:
        near[j, k] = pltpu.make_async_remote_copy(
            src_ref=part_ref.at[block(j, 1 - core, k)],
            dst_ref=near_ref.at[j, pl.ds(k * step, step)],
            send_sem=near_send.at[j * count + k],
            recv_sem=near_recv.at[j * count + k],
            device_id={"exp": sibling},
        )
        near[j, k].start()
    for j, k in order:
        if j == 0:
            continue
        here = pl.ds(k * step, step)
        near[j, k].wait_recv()
        out_ref[j, here] = (
            part_ref[block(j, core, k)].astype(F32) + near_ref[j, here].astype(F32)
        ).astype(BF)
        far[j, k] = pltpu.make_async_remote_copy(
            src_ref=out_ref.at[j, here],
            dst_ref=far_ref.at[j, here],
            send_sem=far_send.at[j * count + k],
            recv_sem=far_recv.at[j * count + k],
            device_id={"exp": lax.rem(chip + j, chips) * 2 + core},
        )
        far[j, k].start()
    for k in range(count):
        here = pl.ds(k * step, step)
        near[0, k].wait_recv()
        total = part_ref[block(0, core, k)].astype(F32) + near_ref[0, here].astype(F32)
        for j in range(1, chips):
            far[j, k].wait_recv()
            total = total + far_ref[j, here].astype(F32)
        finish(k, here, total)
    return list(near.values()) + list(far.values())


def spread_kernel(
    chips, part_ref, tokens_ref, every_ref, hidden_ref, near_ref, out_ref, far_ref,
    near_send, near_recv, far_send, far_recv, share_send, share_recv, cross_send, cross_recv,
):
    me = lax.axis_index("exp")
    core, chip = me % 2, me // 2
    sibling = me + 1 - 2 * core
    rows = tokens_ref.shape[0]
    step = chunk_rows(rows)
    count = rows // step
    enter(me, chips)
    share, cross = {}, {}

    def place(owner, k):
        return pl.ds(pl.multiple_of(owner * rows + k * step, step), step)

    def send(where, j, k, device, send_sem, recv_sem):
        copy = pltpu.make_async_remote_copy(
            src_ref=every_ref.at[where],
            dst_ref=every_ref.at[where],
            send_sem=send_sem.at[j * count + k],
            recv_sem=recv_sem.at[j * count + k],
            device_id={"exp": device},
        )
        copy.start()
        return copy

    def finish(k, here, total):
        hidden = tokens_ref[here].astype(F32) + total
        hidden_ref[here] = hidden
        mine = place(me, k)
        every_ref[mine] = rms_scale(hidden).astype(BF)
        for j in range(1, chips):
            mate = lax.rem(chip + j, chips) * 2 + core
            cross[j, k] = send(mine, j, k, mate, cross_send, cross_recv)
        share[0, k] = send(mine, 0, k, sibling, share_send, share_recv)

    sems = (near_send, near_recv, far_send, far_recv)
    sent = summed_chunks(me, chips, part_ref, near_ref, out_ref, far_ref, sems, finish)
    for k in range(count):
        for j in range(1, chips):
            cross[j, k].wait_recv()
            owner = lax.rem(chip + chips - j, chips) * 2 + core
            share[j, k] = send(place(owner, k), j, k, sibling, share_send, share_recv)
    for copy in share.values():
        copy.wait_recv()
    for copy in sent + list(share.values()) + list(cross.values()):
        copy.wait_send()


def final_kernel(
    chips, part_ref, hidden_ref, result_ref, near_ref, out_ref, far_ref,
    near_send, near_recv, far_send, far_recv,
):
    me = lax.axis_index("exp")
    enter(me, chips)

    def finish(k, here, total):
        result_ref[here] = (hidden_ref[here] + total).astype(BF)

    sems = (near_send, near_recv, far_send, far_recv)
    sent = summed_chunks(me, chips, part_ref, near_ref, out_ref, far_ref, sems, finish)
    for copy in sent:
        copy.wait_send()


def remote_call(kernel, chips, collective_id, groups, out_shape, part, own):
    rows, model = own.shape
    copies = chips * (rows // chunk_rows(rows))
    vmem = pl.BlockSpec(memory_space=pltpu.VMEM)
    return pl.pallas_call(
        partial(kernel, chips),
        in_specs=[vmem, vmem],
        out_specs=jax.tree.map(lambda _: vmem, out_shape),
        out_shape=out_shape,
        scratch_shapes=[pltpu.VMEM((chips, rows, model), BF)] * 3
        + [pltpu.SemaphoreType.DMA((copies,))] * (2 * groups),
        compiler_params=pltpu.CompilerParams(
            collective_id=collective_id, has_side_effects=True, vmem_limit_bytes=48 << 20
        ),
    )(part, own)


def local(
    tokens,
    attend_weight,
    value_weight,
    rate_weight,
    decay_rate,
    output_weight,
    state_cache,
    resume_from,
    expert_index,
    route_weight,
    expert_inner,
    expert_outer,
):
    model = tokens.shape[1]
    value_heads = value_weight.shape[1]
    residual = tokens.astype(F32)
    normed = rms_scale(residual).astype(BF)
    piece = lax.all_gather(normed, "exp", axis=0, tiled=True)

    trajs = state_cache.shape[0]
    replicas = lax.axis_size("rep")
    myself = lax.axis_index("rep")
    my_rows = lax.dynamic_slice_in_dim(resume_from, myself * trajs, trajs)
    listing = resume_from.reshape(replicas, trajs)
    from_me = listing // trajs == myself
    slot_pick = jnp.sum(jnp.where(from_me, listing % trajs, 0), axis=1)
    outgoing = pick_states(state_cache, slot_pick)
    incoming = lax.all_to_all(outgoing, "rep", split_axis=0, concat_axis=0, tiled=True)

    local_experts = expert_inner.shape[0]
    total_experts = lax.axis_size("exp") * local_experts
    numbers = jnp.arange(total_experts, dtype=jnp.int32)
    share = jnp.sum(
        jnp.where(expert_index[None] == numbers[:, None, None], route_weight[None], 0.0), axis=2
    )
    shares = lax.dynamic_slice_in_dim(
        lax.all_gather(share, "exp"), lax.axis_index("exp") * local_experts, local_experts, axis=1
    )
    shares = jnp.moveaxis(shares, 1, 0).reshape(local_experts, -1)

    qk = jnp.dot(piece, attend_weight.reshape(model, -1), preferred_element_type=F32)
    vz = jnp.dot(piece, value_weight.reshape(model, -1), preferred_element_type=F32).astype(BF)
    rate = jnp.dot(piece, rate_weight.reshape(model, -1), preferred_element_type=F32)
    decay_pairs = jnp.repeat(decay_rate, 2)[None, :]
    solved = solve_chunks(trajs, attend_weight.shape[1], value_heads, qk, rate, decay_pairs)
    gated, final_state = apply_states(my_rows // trajs, vz, *solved, incoming)

    output_flat = output_weight.reshape(-1, model)
    partial_rows = jnp.dot(gated, output_flat, preferred_element_type=F32).astype(BF)
    chips = lax.axis_size("exp") // 2
    everyone, hidden = remote_call(
        spread_kernel,
        chips,
        0,
        4,
        [
            jax.ShapeDtypeStruct(partial_rows.shape, BF),
            jax.ShapeDtypeStruct(tokens.shape, F32),
        ],
        partial_rows,
        tokens,
    )
    inner = expert_outer.shape[1]
    weighted = 0.0
    for e in range(local_experts):
        both_parts = jnp.dot(everyone, expert_inner[e], preferred_element_type=F32)
        activated = (jax.nn.silu(both_parts[:, :inner]) * both_parts[:, inner:]).astype(BF)
        produced = jnp.dot(activated, expert_outer[e], preferred_element_type=F32)
        weighted = weighted + shares[e][:, None] * produced
    layer_output = remote_call(
        final_kernel,
        chips,
        1,
        2,
        jax.ShapeDtypeStruct(tokens.shape, BF),
        weighted.astype(BF),
        hidden,
    )
    return (layer_output, final_state)


def solution(mesh):
    in_specs = (
        P(("rep", "exp"), None),
        P(None, "exp", None),
        P(None, "exp", None),
        P(None, "exp", None),
        P("exp"),
        P("exp", None, None),
        P("rep", "exp", None, None),
        P(),
        P(("rep", "exp"), None),
        P(("rep", "exp"), None),
        P("exp", None, None),
        P("exp", None, None),
    )
    out_specs = (P(("rep", "exp"), None), P("rep", "exp", None, None))
    return jax.shard_map(local, mesh=mesh, in_specs=in_specs, out_specs=out_specs, check_vma=False)
```
